32 devices in a mesh: groups: 2 (over y), sector: 16 (over z, x, core).
Axes of the slice: x: 2, y: 2, z: 4, core: 2. Of those that a mesh axis runs over, the one named last changes fastest.
Arguments:
- left_vectors: float32 [32, 128, 128], P(('groups', 'sector')), parts along dimension 0, may hold values from -0.5 to 0.5
- left_cotangent: float32 [32, 128, 128], P(('groups', 'sector')), parts along dimension 0, may hold values from -6 to 6
- gap_inverse: float32 [32, 128, 128], P(('groups', 'sector')), parts along dimension 0, may hold values from -3 to 3
- singular_values: float32 [32, 128], P(('groups', 'sector')), parts along dimension 0, may hold values from 0.5 to 2
- corner: bfloat16 [32, 128, 128], P(('groups', 'sector')), parts along dimension 0, may hold values from -0.5 to 0.5
- sector_sizes: int32 [32], P(('groups', 'sector')), parts along dimension 0, may hold values from 1 to 128, 1024 in all
- edge_t: bfloat16 [32, 8192, 128], P('groups', 'sector'), parts along dimension 0, may hold values from -0.0625 to 0.0625
- right_vectors: bfloat16 [32, 8192, 128], P('groups', 'sector'), parts along dimension 0, may hold values from -0.5 to 0.5
- right_cotangent: bfloat16 [32, 8192, 128], P('groups', 'sector'), parts along dimension 0, may hold values from -4 to 4
Outputs:
- edge_grad: bfloat16 [32, 8192, 128], P('groups', 'sector'), parts along dimension 0
- corner_grad: float32 [32, 128, 128], P(('groups', 'sector')), parts along dimension 0
The draws below stay inside these ranges and needn't reach their ends.
There are 2 independent parts, one for each index of `groups`. The reference program is written for one: setup_inputs(seed, part) draws one part's arguments, and reference() takes and returns one part's arrays. A program takes and returns all parts, laid end to end along the dimension named above; each array names one. Nothing has to cross between parts.
Inputs may be any that keep to these rules, and one draw needn't show every extreme that they name: `sector_sizes`: in each part the live sizes sum to 1024, and some sector has exactly 128.
All inputs are finite; a program needn't handle non-finite values. No bound on the sum of `sector_sizes` on one device may be relied on, other than what follows from the above.
Results may differ from the reference program's by a relative error of at most 0.0057.
Values may be sent and summed in bfloat16 or wider, within the bound.
A program may use at most 128 MiB of HBM per device.

```python
import math
import jax
import jax.numpy as jnp
import numpy as np
from jax import lax

K = 128
NSEC = 16
W = 8192


def levels(rng, extent, split, low, top_value):
    def one(dim, parts):
        draws = jax.random.uniform(jax.random.fold_in(jax.random.fold_in(rng, 6), dim), (parts,), jnp.float32, low / len(split), top_value / len(split))
        return jnp.repeat(jnp.exp(draws), extent[dim] // parts).reshape((-1,) + (1,) * (len(extent) - dim - 1))

    level = one(*split[0])
    for cut in split[1:]:
        level = level * one(*cut)
    return level


def length_profile(amount, total, most, slope):
    loads = [(1 << 20) // math.isqrt(grade ** slope) + 1 for grade in range(2, amount + 1)]
    rest, holding = total - most - (amount - 1), [1] * (amount - 1)
    while rest > 0:
        free = [i for i in range(amount - 1) if holding[i] < most]
        whole, left = sum([loads[i] for i in free]), rest
        for i in free:
            extra = min(most - holding[i], max(1, left * loads[i] // whole), rest)
            holding[i] = holding[i] + extra
            rest = rest - extra
    return np.array([most] + holding)


def uneven(stream_key, count, total, reach, skew):
    if count == 2:
        one = jax.random.randint(stream_key, (), max(1, total - reach), min(reach, total - 1) + 1)
        return jnp.stack([one, total - one])
    tallies = jnp.asarray(length_profile(count, total, reach, skew), jnp.int32)
    twos = (count - 1) // 2
    giver, taker = tallies[1:1 + 2 * twos:2], tallies[2:2 + 2 * twos:2]
    margin = jnp.minimum(giver - 1, reach - taker)
    shifted = jax.random.randint(jax.random.fold_in(stream_key, 1), (twos,), 0, 1 << 20) % (margin + 1)
    tallies = tallies.at[1:1 + 2 * twos:2].set(giver - shifted).at[2:2 + 2 * twos:2].set(taker + shifted)
    return tallies[jax.random.permutation(jax.random.fold_in(stream_key, 2), count)]


def bell_draw(own_key, dims, spread, bound, shards=(), kind=jnp.bfloat16):
    gain = levels(own_key, dims, shards, -0.22, 0.18) if shards else 1.0
    drawn = jax.random.normal(own_key, dims, jnp.float32) * spread * gain
    return jnp.minimum(jnp.maximum(drawn, -bound), bound).astype(kind)


def setup_inputs(seed: int = 0, part: int = 0) -> dict:
    key_of = jax.random.split(jax.random.key(seed), 10)
    part_keys = jax.random.split(jax.random.fold_in(key_of[9], part), 10)
    left_vectors = bell_draw(part_keys[0], (NSEC, K, K), K ** -0.5, 0.5, ((0, 16),), jnp.float32)
    left_cotangent = bell_draw(part_keys[1], (NSEC, K, K), 1.0, 6.0, ((0, 16),), jnp.float32)
    gap_inverse = bell_draw(part_keys[2], (NSEC, K, K), 0.5, 3.0, ((0, 16),), jnp.float32)
    singular_values = jnp.clip(jnp.exp(math.log(2.0) - 1.3862944 * jax.random.uniform(part_keys[3], (NSEC, K), jnp.float32) ** levels(part_keys[3], (NSEC, K), ((0, 16),), -0.2, 0.2)), 0.5, 2.0)
    corner = bell_draw(part_keys[4], (NSEC, K, K), K ** -0.5, 0.5, ((0, 16),))
    sector_sizes = uneven(part_keys[5], NSEC, NSEC * K // 2, K, 0).astype(jnp.int32)
    edge_t = bell_draw(part_keys[6], (NSEC, W, K), W ** -0.5, 0.0625, ((1, 16),))
    right_vectors = bell_draw(part_keys[7], (NSEC, W, K), K ** -0.5, 0.5, ((1, 16),))
    right_cotangent = bell_draw(part_keys[8], (NSEC, W, K), 0.25, 4.0, ((1, 16),))
    return {"left_vectors": left_vectors, "left_cotangent": left_cotangent, "gap_inverse": gap_inverse, "singular_values": singular_values, "corner": corner, "sector_sizes": sector_sizes, "edge_t": edge_t, "right_vectors": right_vectors, "right_cotangent": right_cotangent}


def small_factors(left_vectors, left_cotangent, gap_inverse, singular_values, corner, sector_sizes, inner_sums):
    tile_width = left_vectors.shape[-1]
    position = lax.broadcasted_iota(jnp.int32, (1, tile_width), 1)
    live_rows = (position < sector_sizes[:, None].astype(jnp.int32)).astype(jnp.float32)
    block_mask = live_rows[:, :, None] * live_rows[:, None, :]
    masked_left = left_vectors * block_mask
    masked_cot = left_cotangent * block_mask
    masked_gap = gap_inverse * block_mask
    masked_corner = (corner.astype(jnp.float32) * block_mask).astype(jnp.bfloat16)
    highest = lax.Precision.HIGHEST
    inner_left = jnp.einsum("sji,sjl->sil", masked_left, masked_cot, precision=highest)
    inner_right = inner_sums * block_mask
    sigma_row = singular_values[:, None, :]
    sigma_col = singular_values[:, :, None]
    core_term = masked_gap * (inner_left - jnp.swapaxes(inner_left, 1, 2)) * sigma_row
    core_term = core_term + sigma_col * (masked_gap * (inner_right - jnp.swapaxes(inner_right, 1, 2)))
    inverse = (1.0 / singular_values)[:, None, :]
    scaled = masked_left * inverse
    absorb = jnp.einsum("sij,sjl->sil", masked_left, core_term, precision=highest)
    absorb = absorb + (masked_cot - jnp.einsum("sij,sjl->sil", masked_left, inner_left, precision=highest)) * inverse
    absorb = absorb - jnp.einsum("sij,sjl->sil", scaled, inner_right, precision=highest)
    return absorb.astype(jnp.bfloat16), scaled.astype(jnp.bfloat16), masked_corner, block_mask


def reference(left_vectors, left_cotangent, gap_inverse, singular_values, corner, sector_sizes, edge_t, right_vectors, right_cotangent):
    def inner_one(items):
        vectors, cotangent = items
        return jnp.dot(vectors.T, cotangent, preferred_element_type=jnp.float32)

    inner_sums = lax.map(inner_one, (right_vectors, right_cotangent))
    absorb, scaled, masked_corner, block_mask = small_factors(
        left_vectors, left_cotangent, gap_inverse, singular_values, corner, sector_sizes, inner_sums)

    def apply_one(items):
        vectors, cotangent, edge_block, absorb_one, scaled_one, corner_one, mask_one = items
        projected = jnp.dot(vectors, absorb_one.T, preferred_element_type=jnp.float32)
        projected = projected + jnp.dot(cotangent, scaled_one.T, preferred_element_type=jnp.float32)
        projected = projected.astype(jnp.bfloat16)
        edge_one = jnp.dot(projected, corner_one, preferred_element_type=jnp.float32).astype(jnp.bfloat16)
        corner_sum = jnp.dot(projected.T, edge_block, preferred_element_type=jnp.float32) * mask_one
        return edge_one, corner_sum

    edge_grad, corner_grad = lax.map(apply_one, (right_vectors, right_cotangent, edge_t, absorb, scaled, masked_corner, block_mask))
    return edge_grad, corner_grad
```

```python
import jax
import jax.numpy as jnp
from jax import lax
from jax.experimental import pallas as pl
from jax.experimental.pallas import tpu as pltpu
from jax.sharding import PartitionSpec as P

MESH = pl.DeviceIdType.MESH
HIGHEST = lax.Precision.HIGHEST
F32 = jnp.float32
BF16 = jnp.bfloat16


def grid_of(count):
    chips = count // 2
    wide = 4 if chips > 8 and chips % 4 == 0 else (2 if chips % 2 == 0 else 1)
    return chips // wide, wide


def loop(lower, upper, step):
    if upper - lower <= 4:
        for index in range(lower, upper):
            step(index)
    else:
        lax.fori_loop(lower, upper, lambda i, c: (step(i), c)[1], 0)


def kernel(
    count, Z, X,
    left_ref, cot_ref, gap_ref, sv_ref, corner_ref, size_ref, edge_hbm, vect_hbm, rcot_hbm,
    out_hbm, cgrad_ref,
    vect, rcot, edge, outb,
    gsc, gab,
    i_cs, i_cr, i_xs, i_xr, i_acc, i_zs, i_zr,
    m_cs, m_cr, m_xs, m_xr, m_acc, m_zs, m_zr,
    load_sem, out_sem,
    gsc_z, gsc_x, gsc_c, gsc_r, gab_z, gab_x, gab_c, gab_r,
    i_csem, i_xsem, i_zsem, m_csem, m_xsem, m_zsem,
):
    K = left_ref.shape[-1]
    half = count // 2
    group = lax.axis_index("groups")
    me = lax.axis_index("sector")
    z = me // (2 * X)
    x = (me // 2) % X
    c = me % 2
    sib = me + 1 - 2 * c

    def sector(dz, dx, parity):
        return (lax.rem(z + dz + Z, Z) * X + lax.rem(x + dx + X, X)) * 2 + parity

    def remote(src, dst, ssem, rsem, target):
        return pltpu.make_async_remote_copy(
            src_ref=src, dst_ref=dst, send_sem=ssem, recv_sem=rsem,
            device_id=(group, target), device_id_type=MESH,
        )

    def load(which, t):
        dz = (t + 1) % Z
        first = lax.rem(z + dz, Z) * (2 * X)
        src, dst = ((vect_hbm, vect), (rcot_hbm, rcot), (edge_hbm, edge))[which]
        return pltpu.make_async_copy(
            src.at[pl.ds(first, 2 * X)], dst.at[pl.ds(first, 2 * X)], load_sem.at[which, dz]
        )

    def start_loads(t):
        load(0, t).start()
        load(1, t).start()

    barrier = pltpu.get_barrier_semaphore()

    def greet(target):
        pl.semaphore_signal(barrier, inc=1, device_id=(group, target), device_id_type=MESH)

    loop(1, Z, lambda dz: greet(sector(dz, 0, c)))
    for dx in range(1, X):
        greet(sector(0, dx, c))
    greet(sib)

    loop(0, Z, start_loads)
    loop(0, Z, lambda t: load(2, t).start())

    size = size_ref[0]
    live = (lax.broadcasted_iota(jnp.int32, (K, K), 0) < size) & (
        lax.broadcasted_iota(jnp.int32, (K, K), 1) < size
    )
    mask = jnp.where(live, 1.0, 0.0)
    left = left_ref[0] * mask
    cot = cot_ref[0] * mask
    gap = gap_ref[0] * mask
    sigma_row = jnp.broadcast_to(sv_ref[...], (K, K))
    sigma_col = sigma_row.T
    inv_row = 1.0 / sigma_row
    inv_col = inv_row.T
    scaled = (left * inv_row).astype(BF16)
    gsc[me, 0:K, :] = (left * inv_row).T.astype(BF16)
    gsc[me, K:, :] = (corner_ref[0].astype(F32) * mask).astype(BF16)
    inner_left = jnp.dot(left.T, cot, precision=HIGHEST, preferred_element_type=F32)
    early = gap * (inner_left - inner_left.T) * sigma_row - inner_left * inv_row
    early = jnp.dot(left, early, precision=HIGHEST, preferred_element_type=F32) + cot * inv_row

    pl.semaphore_wait(barrier, (Z - 1) + (X - 1) + 1)

    dims = (((0,), (0,)), ((), ()))

    def inner_part(s):
        return lax.dot_general(vect[s], rcot[s], dims, preferred_element_type=F32)

    def edge_part(s):
        both = jnp.concatenate([vect[s], rcot[s]], axis=1)
        return lax.dot_general(both, edge[s], dims, preferred_element_type=F32)

    def c_copy(send, recv, sem, dz):
        return remote(send.at[dz], recv.at[dz], sem.at[0, dz], sem.at[1, dz], sib)

    def x_copy(send, recv, sem, dz, dx):
        return remote(
            send.at[dz, dx - 1], recv.at[dz, dx - 1],
            sem.at[0, dz, dx - 1], sem.at[1, dz, dx - 1], sector(0, dx, c),
        )

    def z_copy(send, recv, sem, dz):
        return remote(
            send.at[dz - 1], recv.at[dz - 1], sem.at[0, dz - 1], sem.at[1, dz - 1],
            sector(dz, 0, c),
        )

    def core_send(part, send, recv, sem, waits):
        def step(t):
            dz = (t + 1) % Z
            for which in waits:
                load(which, t).wait()
            for dx in range(X):
                send[dz, dx] = part(sector(dz, dx, 1 - c)).astype(BF16)
            c_copy(send, recv, sem, dz).start()
        loop(0, Z, step)

    def x_send(part, bufs, sems):
        cs, cr, xs, xr, acc, zs, zr = bufs
        csem, xsem, zsem = sems

        def step(t):
            dz = (t + 1) % Z
            own = [part(sector(dz, dx, c)) for dx in range(X)]
            c_copy(cs, cr, csem, dz).wait_recv()
            for dx in range(1, X):
                xs[dz, dx - 1] = (own[dx] + cr[dz, dx].astype(F32)).astype(BF16)
                x_copy(xs, xr, xsem, dz, dx).start()
            acc[dz] = own[0] + cr[dz, 0].astype(F32)
        loop(0, Z, step)

    def x_sum(bufs, sems, dz):
        cs, cr, xs, xr, acc, zs, zr = bufs
        total = acc[dz]
        for dx in range(1, X):
            x_copy(xs, xr, sems[1], dz, dx).wait_recv()
            total = total + xr[dz, dx - 1].astype(F32)
        return total

    def z_send(bufs, sems):
        def step(dz):
            bufs[5][dz - 1] = x_sum(bufs, sems, dz).astype(BF16)
            z_copy(bufs[5], bufs[6], sems[2], dz).start()
        loop(1, Z, step)

    def z_sum(bufs, sems):
        acc = bufs[4]
        acc[0] = x_sum(bufs, sems, 0)

        def step(dz):
            z_copy(bufs[5], bufs[6], sems[2], dz).wait_recv()
            acc[0] = acc[0] + bufs[6][dz - 1].astype(F32)
        loop(1, Z, step)
        return acc[0]

    def finish(bufs, sems):
        cs, cr, xs, xr, acc, zs, zr = bufs

        def step(dz):
            c_copy(cs, cr, sems[0], dz).wait_send()
            for dx in range(1, X):
                x_copy(xs, xr, sems[1], dz, dx).wait_send()
        loop(0, Z, step)
        loop(1, Z, lambda dz: z_copy(zs, zr, sems[2], dz).wait_send())

    def g_z(buf, zsem, rsem, dz):
        return remote(buf.at[me], buf.at[me], zsem.at[dz - 1], rsem.at[me], sector(dz, 0, c))

    def g_x(buf, xsem, rsem, dz, dx):
        s = sector(-dz, 0, c)
        return remote(buf.at[s], buf.at[s], xsem.at[dz, dx - 1], rsem.at[s], sector(0, dx, c))

    def g_c(buf, csem, rsem, dz, dx):
        s = sector(-dz, -dx, c)
        return remote(buf.at[s], buf.at[s], csem.at[dz, dx], rsem.at[s], sib)

    def arrived(buf, csem, rsem, s):
        remote(buf.at[s], buf.at[s], csem.at[0, 0], rsem.at[s], sib).wait_recv()

    def g_own(buf, zsem, xsem, csem, rsem):
        loop(1, Z, lambda dz: g_z(buf, zsem, rsem, dz).start())
        for dx in range(1, X):
            g_x(buf, xsem, rsem, 0, dx).start()
        g_c(buf, csem, rsem, 0, 0).start()

    def g_pass_z(buf, xsem, csem, rsem, dz):
        arrived(buf, csem, rsem, sector(-dz, 0, c))
        for dx in range(1, X):
            g_x(buf, xsem, rsem, dz, dx).start()
        g_c(buf, csem, rsem, dz, 0).start()

    def g_pass_x(buf, csem, rsem, dz, dx):
        arrived(buf, csem, rsem, sector(-dz, -dx, c))
        g_c(buf, csem, rsem, dz, dx).start()

    def g_finish(buf, zsem, xsem, csem, rsem):
        loop(1, Z, lambda dz: g_z(buf, zsem, rsem, dz).wait_send())

        def step(dz):
            for dx in range(1, X):
                g_x(buf, xsem, rsem, dz, dx).wait_send()
            for dx in range(X):
                g_c(buf, csem, rsem, dz, dx).wait_send()
        loop(0, Z, step)

    i_bufs, i_sems = (i_cs, i_cr, i_xs, i_xr, i_acc, i_zs, i_zr), (i_csem, i_xsem, i_zsem)
    m_bufs, m_sems = (m_cs, m_cr, m_xs, m_xr, m_acc, m_zs, m_zr), (m_csem, m_xsem, m_zsem)

    core_send(inner_part, i_cs, i_cr, i_csem, (0, 1))
    x_send(inner_part, i_bufs, i_sems)
    g_own(gsc, gsc_z, gsc_x, gsc_c, gsc_r)
    core_send(edge_part, m_cs, m_cr, m_csem, (2,))
    z_send(i_bufs, i_sems)
    x_send(edge_part, m_bufs, m_sems)
    inner_right = z_sum(i_bufs, i_sems) * mask
    late = sigma_col * (gap * (inner_right - inner_right.T)) - inv_col * inner_right
    absorb = early + jnp.dot(left, late, precision=HIGHEST, preferred_element_type=F32)
    gab[me] = absorb.T.astype(BF16)
    g_own(gab, gab_z, gab_x, gab_c, gab_r)

    loop(1, Z, lambda dz: g_pass_z(gsc, gsc_x, gsc_c, gsc_r, dz))

    def gsc_pass(dz):
        for dx in range(1, X):
            g_pass_x(gsc, gsc_c, gsc_r, dz, dx)
    loop(0, Z, gsc_pass)
    z_send(m_bufs, m_sems)

    def out_copy(s):
        return pltpu.make_async_copy(outb.at[s], out_hbm.at[s], out_sem.at[s])

    def project(s):
        both = jnp.concatenate([vect[s], rcot[s]], axis=1)
        factors = jnp.concatenate([gab[s], gsc[s, 0:K, :]], axis=0)
        projected = jnp.dot(both, factors, preferred_element_type=F32).astype(BF16)
        outb[s] = jnp.dot(projected, gsc[s, K:, :], preferred_element_type=F32).astype(BF16)
        out_copy(s).start()

    project(me)
    loop(1, Z, lambda dz: g_pass_z(gab, gab_x, gab_c, gab_r, dz))

    def gab_pass(dz):
        for dx in range(1, X):
            g_pass_x(gab, gab_c, gab_r, dz, dx)
    loop(0, Z, gab_pass)

    def project_mine(dz):
        for dx in range(X):
            s = sector(-dz, -dx, c)
            if not isinstance(dz, int):
                project(s)
            elif dz or dx:
                project(s)
    if Z > 4:
        for dx in range(1, X):
            project(sector(0, -dx, c))
        loop(1, Z, project_mine)
    else:
        loop(0, Z, project_mine)

    def project_other(dz):
        for dx in range(X):
            s = sector(-dz, -dx, 1 - c)
            arrived(gsc, gsc_c, gsc_r, s)
            arrived(gab, gab_c, gab_r, s)
            project(s)
    loop(0, Z, project_other)

    moments = z_sum(m_bufs, m_sems)
    factors = jnp.concatenate([absorb.astype(BF16), scaled], axis=1).astype(F32)
    cgrad_ref[0] = jnp.dot(factors, moments, precision=HIGHEST, preferred_element_type=F32) * mask

    finish(i_bufs, i_sems)
    finish(m_bufs, m_sems)
    g_finish(gsc, gsc_z, gsc_x, gsc_c, gsc_r)
    g_finish(gab, gab_z, gab_x, gab_c, gab_r)
    loop(0, count, lambda s: out_copy(s).wait())


def body(count, *args):
    left, cot, gap, sv, corner, sizes, edge, vect, rcot = args
    Z, X = grid_of(count)
    K = left.shape[-1]
    W = edge.shape[1]

    def sums(rows):
        return [
            pltpu.VMEM((Z, X, rows, K), BF16), pltpu.VMEM((Z, X, rows, K), BF16),
            pltpu.VMEM((Z, X - 1, rows, K), BF16), pltpu.VMEM((Z, X - 1, rows, K), BF16),
            pltpu.VMEM((Z, rows, K), F32),
            pltpu.VMEM((Z - 1, rows, K), BF16), pltpu.VMEM((Z - 1, rows, K), BF16),
        ]

    dma = pltpu.SemaphoreType.DMA
    gather_sems = [dma((Z - 1,)), dma((Z, X - 1)), dma((Z, X)), dma((count,))]
    sum_sems = [dma((2, Z)), dma((2, Z, X - 1)), dma((2, Z - 1))]
    vmem = pl.BlockSpec(memory_space=pltpu.VMEM)
    hbm = pl.BlockSpec(memory_space=pl.ANY)

    def call(*refs):
        return kernel(count, Z, X, *refs)

    return pl.pallas_call(
        call,
        out_shape=(
            jax.ShapeDtypeStruct(edge.shape, BF16),
            jax.ShapeDtypeStruct((1, K, K), F32),
        ),
        in_specs=[vmem] * 5 + [pl.BlockSpec(memory_space=pltpu.SMEM)] + [hbm] * 3,
        out_specs=(hbm, vmem),
        scratch_shapes=[
            pltpu.VMEM((count, W, K), BF16), pltpu.VMEM((count, W, K), BF16),
            pltpu.VMEM((count, W, K), BF16), pltpu.VMEM((count, W, K), BF16),
            pltpu.VMEM((count, 2 * K, K), BF16), pltpu.VMEM((count, K, K), BF16),
            *sums(K), *sums(2 * K),
            dma((3, Z)), dma((count,)),
            *gather_sems, *gather_sems,
            *sum_sems, *sum_sems,
        ],
        compiler_params=pltpu.CompilerParams(
            collective_id=0, has_side_effects=True, vmem_limit_bytes=56 * 1024 * 1024
        ),
        cost_estimate=pl.CostEstimate(
            flops=2 * 6 * count * W * K * K, bytes_accessed=8 * count * W * K, transcendentals=0
        ),
    )(left, cot, gap, sv, corner, sizes, edge, vect, rcot)


def solution(mesh):
    count = mesh.shape["sector"]
    in_specs = (
        P(("groups", "sector"), None, None),
        P(("groups", "sector"), None, None),
        P(("groups", "sector"), None, None),
        P(("groups", "sector"), None),
        P(("groups", "sector"), None, None),
        P(("groups", "sector")),
        P("groups", "sector", None),
        P("groups", "sector", None),
        P("groups", "sector", None),
    )
    out_specs = (P("groups", "sector", None), P(("groups", "sector"), None, None))

    def run(*args):
        return body(count, *args)

    return jax.shard_map(run, mesh=mesh, in_specs=in_specs, out_specs=out_specs, check_vma=False)
```

```python
import jax
import jax.numpy as jnp
from jax import lax
from jax.experimental import pallas as pl
from jax.experimental.pallas import tpu as pltpu
from jax.sharding import PartitionSpec as P

MESH = pl.DeviceIdType.MESH
HIGHEST = lax.Precision.HIGHEST
F32 = jnp.float32
BF16 = jnp.bfloat16


def grid_of(count):
    chips = count // 2
    wide = 4 if chips > 8 and chips % 4 == 0 else (2 if chips % 2 == 0 else 1)
    return chips // wide, wide


def loop(lower, upper, step):
    if upper - lower <= 4:
        for index in range(lower, upper):
            step(index)
    else:
        lax.fori_loop(lower, upper, lambda i, c: (step(i), c)[1], 0)


def kernel(
    count, Z, X,
    left_ref, cot_ref, gap_ref, sv_ref, corner_ref, size_ref, edge_hbm, vect_hbm, rcot_hbm,
    vect, rcot, gsc, gab, own_ref, sums_ref,
    edge,
    i_cs, i_cr, i_xs, i_xr, i_acc, i_zs, i_zr,
    m_cs, m_cr, m_xs, m_xr, m_acc, m_zs, m_zr,
    load_sem,
    gsc_z, gsc_x, gsc_c, gsc_r, gab_z, gab_x, gab_c, gab_r,
    i_csem, i_xsem, i_zsem, m_csem, m_xsem, m_zsem,
):
    K = left_ref.shape[-1]
    half = count // 2
    group = lax.axis_index("groups")
    me = lax.axis_index("sector")
    z = me // (2 * X)
    x = (me // 2) % X
    c = me % 2
    sib = me + 1 - 2 * c

    def sector(dz, dx, parity):
        return (lax.rem(z + dz + Z, Z) * X + lax.rem(x + dx + X, X)) * 2 + parity

    def remote(src, dst, ssem, rsem, target):
        return pltpu.make_async_remote_copy(
            src_ref=src, dst_ref=dst, send_sem=ssem, recv_sem=rsem,
            device_id=(group, target), device_id_type=MESH,
        )

    def load(which, t):
        dz = (t + 1) % Z
        first = lax.rem(z + dz, Z) * (2 * X)
        src, dst = ((vect_hbm, vect), (rcot_hbm, rcot), (edge_hbm, edge))[which]
        return pltpu.make_async_copy(
            src.at[pl.ds(first, 2 * X)], dst.at[pl.ds(first, 2 * X)], load_sem.at[which, dz]
        )

    def start_loads(t):
        load(0, t).start()
        load(1, t).start()

    barrier = pltpu.get_barrier_semaphore()

    def greet(target):
        pl.semaphore_signal(barrier, inc=1, device_id=(group, target), device_id_type=MESH)

    loop(1, Z, lambda dz: greet(sector(dz, 0, c)))
    for dx in range(1, X):
        greet(sector(0, dx, c))
    greet(sib)

    loop(0, Z, start_loads)
    loop(0, Z, lambda t: load(2, t).start())

    size = size_ref[0]
    live = (lax.broadcasted_iota(jnp.int32, (K, K), 0) < size) & (
        lax.broadcasted_iota(jnp.int32, (K, K), 1) < size
    )
    mask = jnp.where(live, 1.0, 0.0)
    left = left_ref[0] * mask
    cot = cot_ref[0] * mask
    gap = gap_ref[0] * mask
    sigma_row = jnp.broadcast_to(sv_ref[...], (K, K))
    sigma_col = sigma_row.T
    inv_row = 1.0 / sigma_row
    inv_col = inv_row.T
    scaled = (left * inv_row).astype(BF16)
    corner = (corner_ref[0].astype(F32) * mask).astype(BF16)
    gsc[me] = lax.dot_general(
        scaled, corner, (((0,), (0,)), ((), ())), preferred_element_type=F32
    ).astype(BF16)
    inner_left = jnp.dot(left.T, cot, precision=HIGHEST, preferred_element_type=F32)
    early = gap * (inner_left - inner_left.T) * sigma_row - inner_left * inv_row
    early = jnp.dot(left, early, precision=HIGHEST, preferred_element_type=F32) + cot * inv_row

    pl.semaphore_wait(barrier, (Z - 1) + (X - 1) + 1)

    dims = (((0,), (0,)), ((), ()))

    def inner_part(s):
        return lax.dot_general(vect[s], rcot[s], dims, preferred_element_type=F32)

    def edge_part(s):
        both = jnp.concatenate([vect[s], rcot[s]], axis=1)
        return lax.dot_general(both, edge[s], dims, preferred_element_type=F32)

    def c_copy(send, recv, sem, dz):
        return remote(send.at[dz], recv.at[dz], sem.at[0, dz], sem.at[1, dz], sib)

    def x_copy(send, recv, sem, dz, dx):
        return remote(
            send.at[dz, dx - 1], recv.at[dz, dx - 1],
            sem.at[0, dz, dx - 1], sem.at[1, dz, dx - 1], sector(0, dx, c),
        )

    def z_copy(send, recv, sem, dz):
        return remote(
            send.at[dz - 1], recv.at[dz - 1], sem.at[0, dz - 1], sem.at[1, dz - 1],
            sector(dz, 0, c),
        )

    def core_send(part, send, recv, sem, waits):
        def step(t):
            dz = (t + 1) % Z
            for which in waits:
                load(which, t).wait()
            for dx in range(X):
                send[dz, dx] = part(sector(dz, dx, 1 - c)).astype(BF16)
            c_copy(send, recv, sem, dz).start()
        loop(0, Z, step)

    def x_send(part, bufs, sems):
        cs, cr, xs, xr, acc, zs, zr = bufs
        csem, xsem, zsem = sems

        def step(t):
            dz = (t + 1) % Z
            own = [part(sector(dz, dx, c)) for dx in range(X)]
            c_copy(cs, cr, csem, dz).wait_recv()
            for dx in range(1, X):
                xs[dz, dx - 1] = (own[dx] + cr[dz, dx].astype(F32)).astype(BF16)
                x_copy(xs, xr, xsem, dz, dx).start()
            acc[dz] = own[0] + cr[dz, 0].astype(F32)
        loop(0, Z, step)

    def x_sum(bufs, sems, dz):
        cs, cr, xs, xr, acc, zs, zr = bufs
        total = acc[dz]
        for dx in range(1, X):
            x_copy(xs, xr, sems[1], dz, dx).wait_recv()
            total = total + xr[dz, dx - 1].astype(F32)
        return total

    def z_send(bufs, sems):
        def step(dz):
            bufs[5][dz - 1] = x_sum(bufs, sems, dz).astype(BF16)
            z_copy(bufs[5], bufs[6], sems[2], dz).start()
        loop(1, Z, step)

    def z_sum(bufs, sems):
        acc = bufs[4]
        acc[0] = x_sum(bufs, sems, 0)

        def step(dz):
            z_copy(bufs[5], bufs[6], sems[2], dz).wait_recv()
            acc[0] = acc[0] + bufs[6][dz - 1].astype(F32)
        loop(1, Z, step)
        return acc[0]

    def finish(bufs, sems):
        cs, cr, xs, xr, acc, zs, zr = bufs

        def step(dz):
            c_copy(cs, cr, sems[0], dz).wait_send()
            for dx in range(1, X):
                x_copy(xs, xr, sems[1], dz, dx).wait_send()
        loop(0, Z, step)
        loop(1, Z, lambda dz: z_copy(zs, zr, sems[2], dz).wait_send())

    def g_z(buf, zsem, rsem, dz):
        return remote(buf.at[me], buf.at[me], zsem.at[dz - 1], rsem.at[me], sector(dz, 0, c))

    def g_x(buf, xsem, rsem, dz, dx):
        s = sector(-dz, 0, c)
        return remote(buf.at[s], buf.at[s], xsem.at[dz, dx - 1], rsem.at[s], sector(0, dx, c))

    def g_c(buf, csem, rsem, dz, dx):
        s = sector(-dz, -dx, c)
        return remote(buf.at[s], buf.at[s], csem.at[dz, dx], rsem.at[s], sib)

    def arrived(buf, csem, rsem, s):
        remote(buf.at[s], buf.at[s], csem.at[0, 0], rsem.at[s], sib).wait_recv()

    def g_own(buf, zsem, xsem, csem, rsem):
        loop(1, Z, lambda dz: g_z(buf, zsem, rsem, dz).start())
        for dx in range(1, X):
            g_x(buf, xsem, rsem, 0, dx).start()
        g_c(buf, csem, rsem, 0, 0).start()

    def g_pass_z(buf, xsem, csem, rsem, dz):
        arrived(buf, csem, rsem, sector(-dz, 0, c))
        for dx in range(1, X):
            g_x(buf, xsem, rsem, dz, dx).start()
        g_c(buf, csem, rsem, dz, 0).start()

    def g_pass_x(buf, csem, rsem, dz, dx):
        arrived(buf, csem, rsem, sector(-dz, -dx, c))
        g_c(buf, csem, rsem, dz, dx).start()

    def g_finish(buf, zsem, xsem, csem, rsem):
        loop(1, Z, lambda dz: g_z(buf, zsem, rsem, dz).wait_send())

        def step(dz):
            for dx in range(1, X):
                g_x(buf, xsem, rsem, dz, dx).wait_send()
            for dx in range(X):
                g_c(buf, csem, rsem, dz, dx).wait_send()
        loop(0, Z, step)

    i_bufs, i_sems = (i_cs, i_cr, i_xs, i_xr, i_acc, i_zs, i_zr), (i_csem, i_xsem, i_zsem)
    m_bufs, m_sems = (m_cs, m_cr, m_xs, m_xr, m_acc, m_zs, m_zr), (m_csem, m_xsem, m_zsem)

    core_send(inner_part, i_cs, i_cr, i_csem, (0, 1))
    x_send(inner_part, i_bufs, i_sems)
    g_own(gsc, gsc_z, gsc_x, gsc_c, gsc_r)
    core_send(edge_part, m_cs, m_cr, m_csem, (2,))
    z_send(i_bufs, i_sems)
    x_send(edge_part, m_bufs, m_sems)
    inner_right = z_sum(i_bufs, i_sems) * mask
    late = sigma_col * (gap * (inner_right - inner_right.T)) - inv_col * inner_right
    absorb = early + jnp.dot(left, late, precision=HIGHEST, preferred_element_type=F32)
    absorb = absorb.astype(BF16)
    gab[me] = lax.dot_general(absorb, corner, dims, preferred_element_type=F32).astype(BF16)
    g_own(gab, gab_z, gab_x, gab_c, gab_r)

    loop(1, Z, lambda dz: g_pass_z(gsc, gsc_x, gsc_c, gsc_r, dz))

    def gsc_pass(dz):
        for dx in range(1, X):
            g_pass_x(gsc, gsc_c, gsc_r, dz, dx)
    loop(0, Z, gsc_pass)
    z_send(m_bufs, m_sems)

    loop(1, Z, lambda dz: g_pass_z(gab, gab_x, gab_c, gab_r, dz))

    def gab_pass(dz):
        for dx in range(1, X):
            g_pass_x(gab, gab_c, gab_r, dz, dx)
    loop(0, Z, gab_pass)

    def others(dz):
        for dx in range(X):
            s = sector(-dz, -dx, 1 - c)
            arrived(gsc, gsc_c, gsc_r, s)
            arrived(gab, gab_c, gab_r, s)
    loop(0, Z, others)

    own_ref[...] = jnp.concatenate([absorb, scaled], axis=1).astype(F32)
    sums_ref[...] = z_sum(m_bufs, m_sems)

    finish(i_bufs, i_sems)
    finish(m_bufs, m_sems)
    g_finish(gsc, gsc_z, gsc_x, gsc_c, gsc_r)
    g_finish(gab, gab_z, gab_x, gab_c, gab_r)


def write_kernel(vect, rcot, gsc, gab, own, sums, size_ref, out_ref, cgrad_ref):
    s = pl.program_id(0)
    both = jnp.concatenate([vect[s], rcot[s]], axis=1)
    factors = jnp.concatenate([gab[s], gsc[s]], axis=0)
    out_ref[0] = jnp.dot(both, factors, preferred_element_type=F32).astype(BF16)

    @pl.when(s == 0)
    def _():
        K = cgrad_ref.shape[-1]
        size = size_ref[0]
        live = (lax.broadcasted_iota(jnp.int32, (K, K), 0) < size) & (
            lax.broadcasted_iota(jnp.int32, (K, K), 1) < size
        )
        grad = jnp.dot(own[...], sums[...], precision=HIGHEST, preferred_element_type=F32)
        cgrad_ref[0] = jnp.where(live, grad, 0.0)


def body(count, *args):
    left, cot, gap, sv, corner, sizes, edge, vect, rcot = args
    Z, X = grid_of(count)
    K = left.shape[-1]
    W = edge.shape[1]

    def sums(rows):
        return [
            pltpu.VMEM((Z, X, rows, K), BF16), pltpu.VMEM((Z, X, rows, K), BF16),
            pltpu.VMEM((Z, X - 1, rows, K), BF16), pltpu.VMEM((Z, X - 1, rows, K), BF16),
            pltpu.VMEM((Z, rows, K), F32),
            pltpu.VMEM((Z - 1, rows, K), BF16), pltpu.VMEM((Z - 1, rows, K), BF16),
        ]

    dma = pltpu.SemaphoreType.DMA
    gather_sems = [dma((Z - 1,)), dma((Z, X - 1)), dma((Z, X)), dma((count,))]
    sum_sems = [dma((2, Z)), dma((2, Z, X - 1)), dma((2, Z - 1))]
    vmem = pl.BlockSpec(memory_space=pltpu.VMEM)
    hbm = pl.BlockSpec(memory_space=pl.ANY)

    def call(*refs):
        return kernel(count, Z, X, *refs)

    flops = 2 * 3 * count * W * K * K
    mib = 1024 * 1024
    limit = 62 * mib - 4 * count * K * (W + K)
    kept = pl.pallas_call(
        call,
        out_shape=(
            pltpu.VMEM((count, W, K), BF16), pltpu.VMEM((count, W, K), BF16),
            pltpu.VMEM((count, K, K), BF16), pltpu.VMEM((count, K, K), BF16),
            pltpu.VMEM((K, 2 * K), F32), pltpu.VMEM((2 * K, K), F32),
        ),
        in_specs=[vmem] * 5 + [pl.BlockSpec(memory_space=pltpu.SMEM)] + [hbm] * 3,
        out_specs=(vmem,) * 6,
        scratch_shapes=[
            pltpu.VMEM((count, W, K), BF16),
            *sums(K), *sums(2 * K),
            dma((3, Z)),
            *gather_sems, *gather_sems,
            *sum_sems, *sum_sems,
        ],
        compiler_params=pltpu.CompilerParams(
            collective_id=0, has_side_effects=True, vmem_limit_bytes=limit
        ),
        cost_estimate=pl.CostEstimate(
            flops=flops, bytes_accessed=6 * count * W * K, transcendentals=0
        ),
    )(left, cot, gap, sv, corner, sizes, edge, vect, rcot)
    return pl.pallas_call(
        write_kernel,
        grid=(count,),
        out_shape=(
            jax.ShapeDtypeStruct(edge.shape, BF16),
            jax.ShapeDtypeStruct((1, K, K), F32),
        ),
        in_specs=[vmem] * 6 + [pl.BlockSpec(memory_space=pltpu.SMEM)],
        out_specs=(
            pl.BlockSpec((1, W, K), lambda s: (s, 0, 0)),
            pl.BlockSpec((1, K, K), lambda s: (0, 0, 0)),
        ),
        compiler_params=pltpu.CompilerParams(vmem_limit_bytes=16 * mib),
        cost_estimate=pl.CostEstimate(
            flops=flops, bytes_accessed=2 * count * W * K, transcendentals=0
        ),
    )(*kept, sizes)


def solution(mesh):
    count = mesh.shape["sector"]
    in_specs = (
        P(("groups", "sector"), None, None),
        P(("groups", "sector"), None, None),
        P(("groups", "sector"), None, None),
        P(("groups", "sector"), None),
        P(("groups", "sector"), None, None),
        P(("groups", "sector")),
        P("groups", "sector", None),
        P("groups", "sector", None),
        P("groups", "sector", None),
    )
    out_specs = (P("groups", "sector", None), P(("groups", "sector"), None, None))

    def run(*args):
        return body(count, *args)

    return jax.shard_map(run, mesh=mesh, in_specs=in_specs, out_specs=out_specs, check_vma=False)
```

```python
import jax
import jax.numpy as jnp
from jax import lax
from jax.experimental import pallas as pl
from jax.experimental.pallas import tpu as pltpu
from jax.sharding import PartitionSpec as P

MESH = pl.DeviceIdType.MESH
HIGHEST = lax.Precision.HIGHEST
F32 = jnp.float32
BF16 = jnp.bfloat16
DIRECT_G = False
DIRECT_A = False
DIRECT_I = True


def grid_of(count):
    chips = count // 2
    wide = 4 if chips > 8 and chips % 4 == 0 else (2 if chips % 2 == 0 else 1)
    return chips // wide, wide


def loop(lower, upper, step, most=4):
    if upper - lower <= most:
        for index in range(lower, upper):
            step(index)
    else:
        lax.fori_loop(lower, upper, lambda i, c: (step(i), c)[1], 0)


def kernel(
    count, Z, X,
    left_ref, cot_ref, gap_ref, sv_ref, corner_ref, size_ref, edge_hbm, vect_hbm, rcot_hbm,
    vect, rcot, gsc, gab, own_ref, sums_ref,
    edge,
    i_cs, i_cr, i_xs, i_xr, i_acc, i_zs, i_zr,
    m_cs, m_cr, m_xs, m_xr, m_acc, m_zs, m_zr,
    load_sem,
    gsc_z, gsc_x, gsc_c, gsc_r, gab_z, gab_x, gab_c, gab_r,
    i_csem, i_xsem, i_zsem, m_csem, m_xsem, m_zsem,
):
    K = left_ref.shape[-1]
    half = count // 2
    group = lax.axis_index("groups")
    me = lax.axis_index("sector")
    z = me // (2 * X)
    x = (me // 2) % X
    c = me % 2
    sib = me + 1 - 2 * c

    def sector(dz, dx, parity):
        return (lax.rem(z + dz + Z, Z) * X + lax.rem(x + dx + X, X)) * 2 + parity

    def remote(src, dst, ssem, rsem, target):
        return pltpu.make_async_remote_copy(
            src_ref=src, dst_ref=dst, send_sem=ssem, recv_sem=rsem,
            device_id=(group, target), device_id_type=MESH,
        )

    def load(which, t):
        dz = (t + 1) % Z
        first = lax.rem(z + dz, Z) * (2 * X)
        src, dst = ((vect_hbm, vect), (rcot_hbm, rcot), (edge_hbm, edge))[which]
        return pltpu.make_async_copy(
            src.at[pl.ds(first, 2 * X)], dst.at[pl.ds(first, 2 * X)], load_sem.at[which, dz]
        )

    def start_loads(t):
        load(0, t).start()
        load(1, t).start()

    barrier = pltpu.get_barrier_semaphore()

    def greet(target):
        pl.semaphore_signal(barrier, inc=1, device_id=(group, target), device_id_type=MESH)

    def greet_row(dz):
        for dx in range(X):
            greet(sector(dz, dx, c))
    for dx in range(1, X):
        greet(sector(0, dx, c))
    loop(1, Z, greet_row)
    greet(sib)

    loop(0, Z, start_loads)
    loop(0, Z, lambda t: load(2, t).start())

    size = size_ref[0]
    live = (lax.broadcasted_iota(jnp.int32, (K, K), 0) < size) & (
        lax.broadcasted_iota(jnp.int32, (K, K), 1) < size
    )
    mask = jnp.where(live, 1.0, 0.0)
    left = left_ref[0] * mask
    cot = cot_ref[0] * mask
    gap = gap_ref[0] * mask
    sigma_row = jnp.broadcast_to(sv_ref[...], (K, K))
    sigma_col = sigma_row.T
    inv_row = 1.0 / sigma_row
    inv_col = inv_row.T
    scaled = (left * inv_row).astype(BF16)
    corner = (corner_ref[0].astype(F32) * mask).astype(BF16)
    gsc[me] = lax.dot_general(
        scaled, corner, (((0,), (0,)), ((), ())), preferred_element_type=F32
    ).astype(BF16)
    inner_left = jnp.dot(left.T, cot, precision=HIGHEST, preferred_element_type=F32)
    early = gap * (inner_left - inner_left.T) * sigma_row - inner_left * inv_row
    early = jnp.dot(left, early, precision=HIGHEST, preferred_element_type=F32) + cot * inv_row

    pl.semaphore_wait(barrier, half)

    dims = (((0,), (0,)), ((), ()))

    def inner_part(s):
        return lax.dot_general(vect[s], rcot[s], dims, preferred_element_type=F32)

    def edge_part(s):
        both = jnp.concatenate([vect[s], rcot[s]], axis=1)
        return lax.dot_general(both, edge[s], dims, preferred_element_type=F32)

    def c_copy(send, recv, sem, dz):
        return remote(send.at[dz], recv.at[dz], sem.at[0, dz], sem.at[1, dz], sib)

    def x_copy(send, recv, sem, dz, dx):
        return remote(
            send.at[dz, dx - 1], recv.at[dz, dx - 1],
            sem.at[0, dz, dx - 1], sem.at[1, dz, dx - 1], sector(0, dx, c),
        )

    def z_copy(send, recv, sem, dz):
        return remote(
            send.at[dz - 1], recv.at[dz - 1], sem.at[0, dz - 1], sem.at[1, dz - 1],
            sector(dz, 0, c),
        )

    def core_send(part, send, recv, sem, waits):
        def step(t):
            dz = (t + 1) % Z
            for which in waits:
                load(which, t).wait()
            for dx in range(X):
                send[dz, dx] = part(sector(dz, dx, 1 - c)).astype(BF16)
            c_copy(send, recv, sem, dz).start()
        loop(0, Z, step)

    def x_send(part, bufs, sems):
        cs, cr, xs, xr, acc, zs, zr = bufs
        csem, xsem, zsem = sems

        def step(t):
            dz = (t + 1) % Z
            own = [part(sector(dz, dx, c)) for dx in range(X)]
            c_copy(cs, cr, csem, dz).wait_recv()
            for dx in range(1, X):
                xs[dz, dx - 1] = (own[dx] + cr[dz, dx].astype(F32)).astype(BF16)
                x_copy(xs, xr, xsem, dz, dx).start()
            acc[dz] = own[0] + cr[dz, 0].astype(F32)
        loop(0, Z, step)

    def x_sum(bufs, sems, dz):
        cs, cr, xs, xr, acc, zs, zr = bufs
        total = acc[dz]
        for dx in range(1, X):
            x_copy(xs, xr, sems[1], dz, dx).wait_recv()
            total = total + xr[dz, dx - 1].astype(F32)
        return total

    def z_send(bufs, sems):
        def step(dz):
            bufs[5][dz - 1] = x_sum(bufs, sems, dz).astype(BF16)
            z_copy(bufs[5], bufs[6], sems[2], dz).start()
        loop(1, Z, step)

    def z_sum(bufs, sems):
        acc = bufs[4]
        acc[0] = x_sum(bufs, sems, 0)

        def step(dz):
            z_copy(bufs[5], bufs[6], sems[2], dz).wait_recv()
            acc[0] = acc[0] + bufs[6][dz - 1].astype(F32)
        loop(1, Z, step)
        return acc[0]

    def finish(bufs, sems):
        cs, cr, xs, xr, acc, zs, zr = bufs

        def step(dz):
            c_copy(cs, cr, sems[0], dz).wait_send()
            for dx in range(1, X):
                x_copy(xs, xr, sems[1], dz, dx).wait_send()
        loop(0, Z, step)
        loop(1, Z, lambda dz: z_copy(zs, zr, sems[2], dz).wait_send())

    def g_z(buf, zsem, rsem, dz):
        return remote(buf.at[me], buf.at[me], zsem.at[dz - 1], rsem.at[me], sector(dz, 0, c))

    def g_x(buf, xsem, rsem, dz, dx):
        s = sector(-dz, 0, c)
        return remote(buf.at[s], buf.at[s], xsem.at[dz, dx - 1], rsem.at[s], sector(0, dx, c))

    def g_c(buf, csem, rsem, dz, dx):
        s = sector(-dz, -dx, c)
        return remote(buf.at[s], buf.at[s], csem.at[dz, dx], rsem.at[s], sib)

    def arrived(buf, csem, rsem, s):
        remote(buf.at[s], buf.at[s], csem.at[0, 0], rsem.at[s], sib).wait_recv()

    def g_own(buf, zsem, xsem, csem, rsem):
        loop(1, Z, lambda dz: g_z(buf, zsem, rsem, dz).start())
        for dx in range(1, X):
            g_x(buf, xsem, rsem, 0, dx).start()
        g_c(buf, csem, rsem, 0, 0).start()

    def others_of(step):
        for dx in range(1, X):
            step(0, dx)

        def row(dz):
            for dx in range(X):
                step(dz, dx)
        loop(1, Z, row)

    def d_g(buf, dsem, rsem, dz, dx):
        return remote(buf.at[me], buf.at[me], dsem.at[dz, dx], rsem.at[me], sector(dz, dx, c))

    def d_own(buf, dsem, csem, rsem):
        others_of(lambda dz, dx: d_g(buf, dsem, rsem, dz, dx).start())
        g_c(buf, csem, rsem, 0, 0).start()

    def d_pass(buf, csem, rsem):
        others_of(lambda dz, dx: g_pass_x(buf, csem, rsem, dz, dx))

    def d_finish(buf, dsem, csem, rsem):
        others_of(lambda dz, dx: d_g(buf, dsem, rsem, dz, dx).wait_send())

        def step(dz):
            for dx in range(X):
                g_c(buf, csem, rsem, dz, dx).wait_send()
        loop(0, Z, step)

    def d_copy(bufs, sem, dz, dx):
        return remote(
            bufs[2].at[dz, dx], bufs[3].at[dz, dx], sem.at[0, dz, dx], sem.at[1, dz, dx],
            sector(dz, dx, c),
        )

    def d_send(part, bufs, sems):
        cs, cr, xs, xr, acc = bufs[:5]

        def step(t):
            dz = (t + 1) % Z
            own = [part(sector(dz, dx, c)) for dx in range(X)]
            c_copy(cs, cr, sems[0], dz).wait_recv()
            for dx in range(X):
                total = own[dx] + cr[dz, dx].astype(F32)
                if dx == 0 and isinstance(t, int) and t == Z - 1:
                    acc[0] = total
                else:
                    xs[dz, dx] = total.astype(BF16)
                    d_copy(bufs, sems[1], dz, dx).start()
        for_last(step)

    def for_last(step):
        loop(0, Z - 1, step)
        step(Z - 1)

    def d_sum(bufs, sems):
        acc = bufs[4]

        def add(dz, dx):
            d_copy(bufs, sems[1], dz, dx).wait_recv()
            acc[0] = acc[0] + bufs[3][dz, dx].astype(F32)
        others_of(add)
        return acc[0]

    def d_done(bufs, sems):
        loop(0, Z, lambda dz: c_copy(bufs[0], bufs[1], sems[0], dz).wait_send())
        others_of(lambda dz, dx: d_copy(bufs, sems[1], dz, dx).wait_send())

    def g_pass_z(buf, xsem, csem, rsem, dz):
        arrived(buf, csem, rsem, sector(-dz, 0, c))
        for dx in range(1, X):
            g_x(buf, xsem, rsem, dz, dx).start()
        g_c(buf, csem, rsem, dz, 0).start()

    def g_pass_x(buf, csem, rsem, dz, dx):
        arrived(buf, csem, rsem, sector(-dz, -dx, c))
        g_c(buf, csem, rsem, dz, dx).start()

    def g_finish(buf, zsem, xsem, csem, rsem):
        loop(1, Z, lambda dz: g_z(buf, zsem, rsem, dz).wait_send())

        def step(dz):
            for dx in range(1, X):
                g_x(buf, xsem, rsem, dz, dx).wait_send()
            for dx in range(X):
                g_c(buf, csem, rsem, dz, dx).wait_send()
        loop(0, Z, step)

    i_bufs, i_sems = (i_cs, i_cr, i_xs, i_xr, i_acc, i_zs, i_zr), (i_csem, i_xsem, i_zsem)
    m_bufs, m_sems = (m_cs, m_cr, m_xs, m_xr, m_acc, m_zs, m_zr), (m_csem, m_xsem, m_zsem)

    core_send(inner_part, i_cs, i_cr, i_csem, (0, 1))
    if DIRECT_I:
        d_send(inner_part, i_bufs, i_sems)
    else:
        x_send(inner_part, i_bufs, i_sems)
    if DIRECT_G:
        d_own(gsc, gsc_z, gsc_c, gsc_r)
    else:
        g_own(gsc, gsc_z, gsc_x, gsc_c, gsc_r)
    core_send(edge_part, m_cs, m_cr, m_csem, (2,))
    if not DIRECT_I:
        z_send(i_bufs, i_sems)
    x_send(edge_part, m_bufs, m_sems)
    inner_right = (d_sum if DIRECT_I else z_sum)(i_bufs, i_sems) * mask
    late = sigma_col * (gap * (inner_right - inner_right.T)) - inv_col * inner_right
    absorb = early + jnp.dot(left, late, precision=HIGHEST, preferred_element_type=F32)
    absorb = absorb.astype(BF16)
    gab[me] = lax.dot_general(absorb, corner, dims, preferred_element_type=F32).astype(BF16)
    if DIRECT_A:
        d_own(gab, gab_z, gab_c, gab_r)
    else:
        g_own(gab, gab_z, gab_x, gab_c, gab_r)

    def pass_on(direct, buf, xsem, csem, rsem):
        if direct:
            d_pass(buf, csem, rsem)
            return
        loop(1, Z, lambda dz: g_pass_z(buf, xsem, csem, rsem, dz))

        def far(dz):
            for dx in range(1, X):
                g_pass_x(buf, csem, rsem, dz, dx)
        loop(0, Z, far)

    pass_on(DIRECT_G, gsc, gsc_x, gsc_c, gsc_r)
    z_send(m_bufs, m_sems)
    pass_on(DIRECT_A, gab, gab_x, gab_c, gab_r)

    def others(dz):
        for dx in range(X):
            s = sector(-dz, -dx, 1 - c)
            arrived(gsc, gsc_c, gsc_r, s)
            arrived(gab, gab_c, gab_r, s)
    loop(0, Z, others)

    own_ref[...] = jnp.concatenate([absorb, scaled], axis=1).astype(F32)
    sums_ref[...] = z_sum(m_bufs, m_sems)

    (d_done if DIRECT_I else finish)(i_bufs, i_sems)
    finish(m_bufs, m_sems)
    if DIRECT_G:
        d_finish(gsc, gsc_z, gsc_c, gsc_r)
    else:
        g_finish(gsc, gsc_z, gsc_x, gsc_c, gsc_r)
    if DIRECT_A:
        d_finish(gab, gab_z, gab_c, gab_r)
    else:
        g_finish(gab, gab_z, gab_x, gab_c, gab_r)


def write_kernel(vect, rcot, gsc, gab, own, sums, size_ref, out_hbm, cgrad_ref, outb, sem):
    def out_copy(s):
        return pltpu.make_async_copy(outb.at[s], out_hbm.at[s], sem.at[s])

    def project(s):
        both = jnp.concatenate([vect[s], rcot[s]], axis=1)
        factors = jnp.concatenate([gab[s], gsc[s]], axis=0)
        outb[s] = jnp.dot(both, factors, preferred_element_type=F32).astype(BF16)
        out_copy(s).start()

    count = vect.shape[0]
    loop(0, count, project, 16)
    K = cgrad_ref.shape[-1]
    size = size_ref[0]
    live = (lax.broadcasted_iota(jnp.int32, (K, K), 0) < size) & (
        lax.broadcasted_iota(jnp.int32, (K, K), 1) < size
    )
    grad = jnp.dot(own[...], sums[...], precision=HIGHEST, preferred_element_type=F32)
    cgrad_ref[0] = jnp.where(live, grad, 0.0)
    loop(0, count, lambda s: out_copy(s).wait(), 16)


def body(count, *args):
    left, cot, gap, sv, corner, sizes, edge, vect, rcot = args
    Z, X = grid_of(count)
    K = left.shape[-1]
    W = edge.shape[1]

    def sums(rows, direct):
        wide = X if direct else X - 1
        return [
            pltpu.VMEM((Z, X, rows, K), BF16), pltpu.VMEM((Z, X, rows, K), BF16),
            pltpu.VMEM((Z, wide, rows, K), BF16), pltpu.VMEM((Z, wide, rows, K), BF16),
            pltpu.VMEM((Z, rows, K), F32),
            pltpu.VMEM((Z - 1, rows, K), BF16), pltpu.VMEM((Z - 1, rows, K), BF16),
        ]

    dma = pltpu.SemaphoreType.DMA
    def gather_sems(direct):
        return [dma((Z, X) if direct else (Z - 1,)), dma((Z, X - 1)), dma((Z, X)), dma((count,))]

    def sum_sems(direct):
        return [dma((2, Z)), dma((2, Z, X if direct else X - 1)), dma((2, Z - 1))]
    vmem = pl.BlockSpec(memory_space=pltpu.VMEM)
    hbm = pl.BlockSpec(memory_space=pl.ANY)

    def call(*refs):
        return kernel(count, Z, X, *refs)

    flops = 2 * 3 * count * W * K * K
    mib = 1024 * 1024
    limit = 62 * mib - 4 * count * K * (W + K)
    kept = pl.pallas_call(
        call,
        out_shape=(
            pltpu.VMEM((count, W, K), BF16), pltpu.VMEM((count, W, K), BF16),
            pltpu.VMEM((count, K, K), BF16), pltpu.VMEM((count, K, K), BF16),
            pltpu.VMEM((K, 2 * K), F32), pltpu.VMEM((2 * K, K), F32),
        ),
        in_specs=[vmem] * 5 + [pl.BlockSpec(memory_space=pltpu.SMEM)] + [hbm] * 3,
        out_specs=(vmem,) * 6,
        scratch_shapes=[
            pltpu.VMEM((count, W, K), BF16),
            *sums(K, DIRECT_I), *sums(2 * K, False),
            dma((3, Z)),
            *gather_sems(DIRECT_G), *gather_sems(DIRECT_A),
            *sum_sems(DIRECT_I), *sum_sems(False),
        ],
        compiler_params=pltpu.CompilerParams(
            collective_id=0, has_side_effects=True, vmem_limit_bytes=limit
        ),
        cost_estimate=pl.CostEstimate(
            flops=flops, bytes_accessed=6 * count * W * K, transcendentals=0
        ),
    )(left, cot, gap, sv, corner, sizes, edge, vect, rcot)
    return pl.pallas_call(
        write_kernel,
        out_shape=(
            jax.ShapeDtypeStruct(edge.shape, BF16),
            jax.ShapeDtypeStruct((1, K, K), F32),
        ),
        in_specs=[vmem] * 6 + [pl.BlockSpec(memory_space=pltpu.SMEM)],
        out_specs=(hbm, vmem),
        scratch_shapes=[pltpu.VMEM((count, W, K), BF16), dma((count,))],
        compiler_params=pltpu.CompilerParams(vmem_limit_bytes=16 * mib),
        cost_estimate=pl.CostEstimate(
            flops=flops, bytes_accessed=2 * count * W * K, transcendentals=0
        ),
    )(*kept, sizes)


def solution(mesh):
    count = mesh.shape["sector"]
    in_specs = (
        P(("groups", "sector"), None, None),
        P(("groups", "sector"), None, None),
        P(("groups", "sector"), None, None),
        P(("groups", "sector"), None),
        P(("groups", "sector"), None, None),
        P(("groups", "sector")),
        P("groups", "sector", None),
        P("groups", "sector", None),
        P("groups", "sector", None),
    )
    out_specs = (P("groups", "sector", None), P(("groups", "sector"), None, None))

    def run(*args):
        return body(count, *args)

    return jax.shard_map(run, mesh=mesh, in_specs=in_specs, out_specs=out_specs, check_vma=False)
```

```python
import jax
import jax.numpy as jnp
from jax import lax
from jax.experimental import pallas as pl
from jax.experimental.pallas import tpu as pltpu
from jax.sharding import PartitionSpec as P

MESH = pl.DeviceIdType.MESH
HIGHEST = lax.Precision.HIGHEST
F32 = jnp.float32
BF16 = jnp.bfloat16
DIRECT_G = False
DIRECT_A = False
DIRECT_I = True


def grid_of(count):
    chips = count // 2
    wide = 4 if chips > 8 and chips % 4 == 0 else (2 if chips % 2 == 0 else 1)
    return chips // wide, wide


def loop(lower, upper, step, most=4):
    if upper - lower <= most:
        for index in range(lower, upper):
            step(index)
    else:
        lax.fori_loop(lower, upper, lambda i, c: (step(i), c)[1], 0)


def kernel(
    count, Z, X,
    left_ref, cot_ref, gap_ref, sv_ref, corner_ref, size_ref, edge_hbm, vect_hbm, rcot_hbm,
    vect, rcot, gsc, gab, own_ref, sums_ref,
    edge,
    i_cs, i_cr, i_xs, i_xr, i_acc, i_zs, i_zr,
    m_cs, m_cr, m_xs, m_xr, m_acc, m_zs, m_zr,
    load_sem,
    gsc_z, gsc_x, gsc_c, gsc_r, gab_z, gab_x, gab_c, gab_r,
    i_csem, i_xsem, i_zsem, m_csem, m_xsem, m_zsem,
):
    K = left_ref.shape[-1]
    half = count // 2
    group = lax.axis_index("groups")
    me = lax.axis_index("sector")
    z = me // (2 * X)
    x = (me // 2) % X
    c = me % 2
    sib = me + 1 - 2 * c

    def sector(dz, dx, parity):
        return (lax.rem(z + dz + Z, Z) * X + lax.rem(x + dx + X, X)) * 2 + parity

    def remote(src, dst, ssem, rsem, target):
        return pltpu.make_async_remote_copy(
            src_ref=src, dst_ref=dst, send_sem=ssem, recv_sem=rsem,
            device_id=(group, target), device_id_type=MESH,
        )

    def load(which, t):
        dz = (t + 1) % Z
        first = lax.rem(z + dz, Z) * (2 * X)
        src, dst = ((vect_hbm, vect), (rcot_hbm, rcot), (edge_hbm, edge))[which]
        return pltpu.make_async_copy(
            src.at[pl.ds(first, 2 * X)], dst.at[pl.ds(first, 2 * X)], load_sem.at[which, dz]
        )

    def start_loads(t):
        load(0, t).start()
        load(1, t).start()

    barrier = pltpu.get_barrier_semaphore()

    def greet(target):
        pl.semaphore_signal(barrier, inc=1, device_id=(group, target), device_id_type=MESH)

    def greet_row(dz):
        for dx in range(X):
            greet(sector(dz, dx, c))
    for dx in range(1, X):
        greet(sector(0, dx, c))
    loop(1, Z, greet_row)
    greet(sib)

    loop(0, Z, start_loads)
    loop(0, Z, lambda t: load(2, t).start())

    size = size_ref[0]
    live = (lax.broadcasted_iota(jnp.int32, (K, K), 0) < size) & (
        lax.broadcasted_iota(jnp.int32, (K, K), 1) < size
    )
    mask = jnp.where(live, 1.0, 0.0)
    left = left_ref[0] * mask
    cot = cot_ref[0] * mask
    gap = gap_ref[0] * mask
    sigma_row = jnp.broadcast_to(sv_ref[...], (K, K))
    sigma_col = sigma_row.T
    inv_row = 1.0 / sigma_row
    inv_col = inv_row.T
    scaled = (left * inv_row).astype(BF16)
    corner = (corner_ref[0].astype(F32) * mask).astype(BF16)
    gsc[me] = lax.dot_general(
        scaled, corner, (((0,), (0,)), ((), ())), preferred_element_type=F32
    ).astype(BF16)
    inner_left = jnp.dot(left.T, cot, precision=HIGHEST, preferred_element_type=F32)
    early = gap * (inner_left - inner_left.T) * sigma_row - inner_left * inv_row
    early = jnp.dot(left, early, precision=HIGHEST, preferred_element_type=F32) + cot * inv_row

    pl.semaphore_wait(barrier, half)

    dims = (((0,), (0,)), ((), ()))

    def inner_part(s):
        return lax.dot_general(vect[s], rcot[s], dims, preferred_element_type=F32)

    def edge_part(s):
        both = jnp.concatenate([vect[s], rcot[s]], axis=1)
        return lax.dot_general(both, edge[s], dims, preferred_element_type=F32)

    def c_copy(send, recv, sem, dz):
        return remote(send.at[dz], recv.at[dz], sem.at[0, dz], sem.at[1, dz], sib)

    def x_copy(send, recv, sem, dz, dx):
        return remote(
            send.at[dz, dx - 1], recv.at[dz, dx - 1],
            sem.at[0, dz, dx - 1], sem.at[1, dz, dx - 1], sector(0, dx, c),
        )

    def z_copy(send, recv, sem, dz):
        return remote(
            send.at[dz - 1], recv.at[dz - 1], sem.at[0, dz - 1], sem.at[1, dz - 1],
            sector(dz, 0, c),
        )

    def core_send(part, send, recv, sem, waits):
        def step(t):
            dz = (t + 1) % Z
            for which in waits:
                load(which, t).wait()
            for dx in range(X):
                send[dz, dx] = part(sector(dz, dx, 1 - c)).astype(BF16)
            c_copy(send, recv, sem, dz).start()
        loop(0, Z, step)

    def x_send(part, bufs, sems):
        cs, cr, xs, xr, acc, zs, zr = bufs
        csem, xsem, zsem = sems

        def step(t):
            dz = (t + 1) % Z
            own = [part(sector(dz, dx, c)) for dx in range(X)]
            c_copy(cs, cr, csem, dz).wait_recv()
            for dx in range(1, X):
                xs[dz, dx - 1] = (own[dx] + cr[dz, dx].astype(F32)).astype(BF16)
                x_copy(xs, xr, xsem, dz, dx).start()
            acc[dz] = own[0] + cr[dz, 0].astype(F32)
        loop(0, Z, step)

    def x_sum(bufs, sems, dz):
        cs, cr, xs, xr, acc, zs, zr = bufs
        total = acc[dz]
        for dx in range(1, X):
            x_copy(xs, xr, sems[1], dz, dx).wait_recv()
            total = total + xr[dz, dx - 1].astype(F32)
        return total

    def z_send(bufs, sems):
        def step(dz):
            bufs[5][dz - 1] = x_sum(bufs, sems, dz).astype(BF16)
            z_copy(bufs[5], bufs[6], sems[2], dz).start()
        loop(1, Z, step)

    def z_sum(bufs, sems):
        acc = bufs[4]
        acc[0] = x_sum(bufs, sems, 0)

        def step(dz):
            z_copy(bufs[5], bufs[6], sems[2], dz).wait_recv()
            acc[0] = acc[0] + bufs[6][dz - 1].astype(F32)
        loop(1, Z, step)
        return acc[0]

    def finish(bufs, sems):
        cs, cr, xs, xr, acc, zs, zr = bufs

        def step(dz):
            c_copy(cs, cr, sems[0], dz).wait_send()
            for dx in range(1, X):
                x_copy(xs, xr, sems[1], dz, dx).wait_send()
        loop(0, Z, step)
        loop(1, Z, lambda dz: z_copy(zs, zr, sems[2], dz).wait_send())

    def g_z(buf, zsem, rsem, dz):
        return remote(buf.at[me], buf.at[me], zsem.at[dz - 1], rsem.at[me], sector(dz, 0, c))

    def g_x(buf, xsem, rsem, dz, dx):
        s = sector(-dz, 0, c)
        return remote(buf.at[s], buf.at[s], xsem.at[dz, dx - 1], rsem.at[s], sector(0, dx, c))

    def g_c(buf, csem, rsem, dz, dx):
        s = sector(-dz, -dx, c)
        return remote(buf.at[s], buf.at[s], csem.at[dz, dx], rsem.at[s], sib)

    def arrived(buf, csem, rsem, s):
        remote(buf.at[s], buf.at[s], csem.at[0, 0], rsem.at[s], sib).wait_recv()

    def g_own(buf, zsem, xsem, csem, rsem):
        loop(1, Z, lambda dz: g_z(buf, zsem, rsem, dz).start())
        for dx in range(1, X):
            g_x(buf, xsem, rsem, 0, dx).start()
        g_c(buf, csem, rsem, 0, 0).start()

    def others_of(step):
        for dx in range(1, X):
            step(0, dx)

        def row(dz):
            for dx in range(X):
                step(dz, dx)
        loop(1, Z, row)

    def d_g(buf, dsem, rsem, dz, dx):
        return remote(buf.at[me], buf.at[me], dsem.at[dz, dx], rsem.at[me], sector(dz, dx, c))

    def d_own(buf, dsem, csem, rsem):
        others_of(lambda dz, dx: d_g(buf, dsem, rsem, dz, dx).start())
        g_c(buf, csem, rsem, 0, 0).start()

    def d_pass(buf, csem, rsem):
        others_of(lambda dz, dx: g_pass_x(buf, csem, rsem, dz, dx))

    def d_finish(buf, dsem, csem, rsem):
        others_of(lambda dz, dx: d_g(buf, dsem, rsem, dz, dx).wait_send())

        def step(dz):
            for dx in range(X):
                g_c(buf, csem, rsem, dz, dx).wait_send()
        loop(0, Z, step)

    def d_copy(bufs, sem, dz, dx):
        return remote(
            bufs[2].at[dz, dx], bufs[3].at[dz, dx], sem.at[0, dz, dx], sem.at[1, dz, dx],
            sector(dz, dx, c),
        )

    def d_send(part, bufs, sems):
        cs, cr, xs, xr, acc = bufs[:5]

        def step(t):
            dz = (t + 1) % Z
            own = [part(sector(dz, dx, c)) for dx in range(X)]
            c_copy(cs, cr, sems[0], dz).wait_recv()
            for dx in range(X):
                total = own[dx] + cr[dz, dx].astype(F32)
                if dx == 0 and isinstance(t, int) and t == Z - 1:
                    acc[0] = total
                else:
                    xs[dz, dx] = total.astype(BF16)
                    d_copy(bufs, sems[1], dz, dx).start()
        for_last(step)

    def for_last(step):
        loop(0, Z - 1, step)
        step(Z - 1)

    def d_sum(bufs, sems):
        acc = bufs[4]

        def add(dz, dx):
            d_copy(bufs, sems[1], dz, dx).wait_recv()
            acc[0] = acc[0] + bufs[3][dz, dx].astype(F32)
        others_of(add)
        return acc[0]

    def d_done(bufs, sems):
        loop(0, Z, lambda dz: c_copy(bufs[0], bufs[1], sems[0], dz).wait_send())
        others_of(lambda dz, dx: d_copy(bufs, sems[1], dz, dx).wait_send())

    def g_pass_z(buf, xsem, csem, rsem, dz):
        arrived(buf, csem, rsem, sector(-dz, 0, c))
        for dx in range(1, X):
            g_x(buf, xsem, rsem, dz, dx).start()
        g_c(buf, csem, rsem, dz, 0).start()

    def g_pass_x(buf, csem, rsem, dz, dx):
        arrived(buf, csem, rsem, sector(-dz, -dx, c))
        g_c(buf, csem, rsem, dz, dx).start()

    def g_finish(buf, zsem, xsem, csem, rsem):
        loop(1, Z, lambda dz: g_z(buf, zsem, rsem, dz).wait_send())

        def step(dz):
            for dx in range(1, X):
                g_x(buf, xsem, rsem, dz, dx).wait_send()
            for dx in range(X):
                g_c(buf, csem, rsem, dz, dx).wait_send()
        loop(0, Z, step)

    i_bufs, i_sems = (i_cs, i_cr, i_xs, i_xr, i_acc, i_zs, i_zr), (i_csem, i_xsem, i_zsem)
    m_bufs, m_sems = (m_cs, m_cr, m_xs, m_xr, m_acc, m_zs, m_zr), (m_csem, m_xsem, m_zsem)

    core_send(inner_part, i_cs, i_cr, i_csem, (0, 1))
    if DIRECT_I:
        d_send(inner_part, i_bufs, i_sems)
    else:
        x_send(inner_part, i_bufs, i_sems)
    if DIRECT_G:
        d_own(gsc, gsc_z, gsc_c, gsc_r)
    else:
        g_own(gsc, gsc_z, gsc_x, gsc_c, gsc_r)
    core_send(edge_part, m_cs, m_cr, m_csem, (2,))
    if not DIRECT_I:
        z_send(i_bufs, i_sems)
    x_send(edge_part, m_bufs, m_sems)
    inner_right = (d_sum if DIRECT_I else z_sum)(i_bufs, i_sems) * mask
    late = sigma_col * (gap * (inner_right - inner_right.T)) - inv_col * inner_right
    absorb = early + jnp.dot(left, late, precision=HIGHEST, preferred_element_type=F32)
    absorb = absorb.astype(BF16)
    gab[me] = lax.dot_general(absorb, corner, dims, preferred_element_type=F32).astype(BF16)
    if DIRECT_A:
        d_own(gab, gab_z, gab_c, gab_r)
    else:
        g_own(gab, gab_z, gab_x, gab_c, gab_r)

    def pass_on(direct, buf, xsem, csem, rsem):
        if direct:
            d_pass(buf, csem, rsem)
            return
        loop(1, Z, lambda dz: g_pass_z(buf, xsem, csem, rsem, dz))

        def far(dz):
            for dx in range(1, X):
                g_pass_x(buf, csem, rsem, dz, dx)
        loop(0, Z, far)

    z_send(m_bufs, m_sems)
    pass_on(DIRECT_G, gsc, gsc_x, gsc_c, gsc_r)
    pass_on(DIRECT_A, gab, gab_x, gab_c, gab_r)

    def others(dz):
        for dx in range(X):
            s = sector(-dz, -dx, 1 - c)
            arrived(gsc, gsc_c, gsc_r, s)
            arrived(gab, gab_c, gab_r, s)
    loop(0, Z, others)

    own_ref[...] = jnp.concatenate([absorb, scaled], axis=1).astype(F32)
    sums_ref[...] = z_sum(m_bufs, m_sems)

    (d_done if DIRECT_I else finish)(i_bufs, i_sems)
    finish(m_bufs, m_sems)
    if DIRECT_G:
        d_finish(gsc, gsc_z, gsc_c, gsc_r)
    else:
        g_finish(gsc, gsc_z, gsc_x, gsc_c, gsc_r)
    if DIRECT_A:
        d_finish(gab, gab_z, gab_c, gab_r)
    else:
        g_finish(gab, gab_z, gab_x, gab_c, gab_r)


def write_kernel(vect, rcot, gsc, gab, own, sums, size_ref, out_hbm, cgrad_ref, outb, sem):
    def out_copy(s):
        return pltpu.make_async_copy(outb.at[s], out_hbm.at[s], sem.at[s])

    def project(s):
        both = jnp.concatenate([vect[s], rcot[s]], axis=1)
        factors = jnp.concatenate([gab[s], gsc[s]], axis=0)
        outb[s] = jnp.dot(both, factors, preferred_element_type=F32).astype(BF16)
        out_copy(s).start()

    count = vect.shape[0]
    loop(0, count, project, 16)
    K = cgrad_ref.shape[-1]
    size = size_ref[0]
    live = (lax.broadcasted_iota(jnp.int32, (K, K), 0) < size) & (
        lax.broadcasted_iota(jnp.int32, (K, K), 1) < size
    )
    grad = jnp.dot(own[...], sums[...], precision=HIGHEST, preferred_element_type=F32)
    cgrad_ref[0] = jnp.where(live, grad, 0.0)
    loop(0, count, lambda s: out_copy(s).wait(), 16)


def body(count, *args):
    left, cot, gap, sv, corner, sizes, edge, vect, rcot = args
    Z, X = grid_of(count)
    K = left.shape[-1]
    W = edge.shape[1]

    def sums(rows, direct):
        wide = X if direct else X - 1
        return [
            pltpu.VMEM((Z, X, rows, K), BF16), pltpu.VMEM((Z, X, rows, K), BF16),
            pltpu.VMEM((Z, wide, rows, K), BF16), pltpu.VMEM((Z, wide, rows, K), BF16),
            pltpu.VMEM((Z, rows, K), F32),
            pltpu.VMEM((Z - 1, rows, K), BF16), pltpu.VMEM((Z - 1, rows, K), BF16),
        ]

    dma = pltpu.SemaphoreType.DMA
    def gather_sems(direct):
        return [dma((Z, X) if direct else (Z - 1,)), dma((Z, X - 1)), dma((Z, X)), dma((count,))]

    def sum_sems(direct):
        return [dma((2, Z)), dma((2, Z, X if direct else X - 1)), dma((2, Z - 1))]
    vmem = pl.BlockSpec(memory_space=pltpu.VMEM)
    hbm = pl.BlockSpec(memory_space=pl.ANY)

    def call(*refs):
        return kernel(count, Z, X, *refs)

    flops = 2 * 3 * count * W * K * K
    mib = 1024 * 1024
    limit = 62 * mib - 4 * count * K * (W + K)
    kept = pl.pallas_call(
        call,
        out_shape=(
            pltpu.VMEM((count, W, K), BF16), pltpu.VMEM((count, W, K), BF16),
            pltpu.VMEM((count, K, K), BF16), pltpu.VMEM((count, K, K), BF16),
            pltpu.VMEM((K, 2 * K), F32), pltpu.VMEM((2 * K, K), F32),
        ),
        in_specs=[vmem] * 5 + [pl.BlockSpec(memory_space=pltpu.SMEM)] + [hbm] * 3,
        out_specs=(vmem,) * 6,
        scratch_shapes=[
            pltpu.VMEM((count, W, K), BF16),
            *sums(K, DIRECT_I), *sums(2 * K, False),
            dma((3, Z)),
            *gather_sems(DIRECT_G), *gather_sems(DIRECT_A),
            *sum_sems(DIRECT_I), *sum_sems(False),
        ],
        compiler_params=pltpu.CompilerParams(
            collective_id=0, has_side_effects=True, vmem_limit_bytes=limit
        ),
        cost_estimate=pl.CostEstimate(
            flops=flops, bytes_accessed=6 * count * W * K, transcendentals=0
        ),
    )(left, cot, gap, sv, corner, sizes, edge, vect, rcot)
    return pl.pallas_call(
        write_kernel,
        out_shape=(
            jax.ShapeDtypeStruct(edge.shape, BF16),
            jax.ShapeDtypeStruct((1, K, K), F32),
        ),
        in_specs=[vmem] * 6 + [pl.BlockSpec(memory_space=pltpu.SMEM)],
        out_specs=(hbm, vmem),
        scratch_shapes=[pltpu.VMEM((count, W, K), BF16), dma((count,))],
        compiler_params=pltpu.CompilerParams(vmem_limit_bytes=16 * mib),
        cost_estimate=pl.CostEstimate(
            flops=flops, bytes_accessed=2 * count * W * K, transcendentals=0
        ),
    )(*kept, sizes)


def solution(mesh):
    count = mesh.shape["sector"]
    in_specs = (
        P(("groups", "sector"), None, None),
        P(("groups", "sector"), None, None),
        P(("groups", "sector"), None, None),
        P(("groups", "sector"), None),
        P(("groups", "sector"), None, None),
        P(("groups", "sector")),
        P("groups", "sector", None),
        P("groups", "sector", None),
        P("groups", "sector", None),
    )
    out_specs = (P("groups", "sector", None), P(("groups", "sector"), None, None))

    def run(*args):
        return body(count, *args)

    return jax.shard_map(run, mesh=mesh, in_specs=in_specs, out_specs=out_specs, check_vma=False)
```
